256 devices in a mesh: dp: 16 (over y, x_lo, core), grad: 16 (over x_hi, z).
Axes of the slice: x: 4 (x_hi: 2, x_lo: 2; x = x_hi * 2 + x_lo), y: 4, z: 8, core: 2. Of those that a mesh axis runs over, the one named last changes fastest.
Arguments:
- acts: bfloat16 [1, 32768, 2560], P(None, 'dp', 'grad'), may hold values from -6 to 6
- out_grads: bfloat16 [1, 32768, 2560], P(None, 'dp', 'grad'), may hold values from -6 to 6
- factor_in: float32 [1, 2560, 2560], P(None, 'dp', 'grad'), may hold values from -3 to 3
- factor_out: float32 [1, 2560, 2560], P(None, 'dp', 'grad'), may hold values from -3 to 3
- basis_in: bfloat16 [1, 2560, 2560], P(None, 'dp'), may hold values from -0.125 to 0.125
- basis_out: bfloat16 [1, 2560, 2560], P(None, 'grad'), may hold values from -0.125 to 0.125
- eig_in: float32 [1, 2560], P(None, 'dp'), may hold values from 0.01 to 1
- eig_out: float32 [1, 2560], P(None, 'grad'), may hold values from 0.01 to 1
Outputs:
- new_factor_in: float32 [1, 2560, 2560], P(None, 'dp', 'grad')
- new_factor_out: float32 [1, 2560, 2560], P(None, 'dp', 'grad')
- precond: bfloat16 [1, 2560, 2560], P(None, 'dp', 'grad')
The draws below stay inside these ranges and needn't reach their ends.
All inputs are finite; a program needn't handle non-finite values.
Results may differ from the reference program's by a relative error of at most 0.009.
Values may be sent and summed in bfloat16 or wider, within the bound.
No kernel may reach another device: no remote copies, remote signals or barrier semaphores. Data moves between devices by JAX's collectives and lax.ppermute only.
A program may use at most 128 MiB of HBM per device.

```python
import math
import jax
import jax.numpy as jnp
from jax import lax

D = 2560
LAYERS = 1
TOKENS = 32768


def level_of(own_key, dims, shards, low, largest):
    def one(position, shards_of):
        draws = jax.random.uniform(jax.random.fold_in(jax.random.fold_in(own_key, 6), position), (shards_of,), jnp.float32, low / len(shards), largest / len(shards))
        return jnp.repeat(jnp.exp(draws), dims[position] // shards_of).reshape((-1,) + (1,) * (len(dims) - position - 1))

    loudness = one(*shards[0])
    for cut in shards[1:]:
        loudness = loudness * one(*cut)
    return loudness


def scatter_about(rng, extent, spread, bound, split=(), held_as=jnp.bfloat16):
    drawn = spread * jax.random.normal(rng, extent, jnp.float32)
    if split:
        drawn = drawn * level_of(rng, extent, split, -0.22, 0.18)
    return jnp.clip(drawn, -bound, bound).astype(held_as)


def setup_inputs(seed: int = 0) -> dict:
    key_of = jax.random.split(jax.random.key(seed), 9)
    return {
        "acts": scatter_about(key_of[0], (LAYERS, TOKENS, D), 1.0, 6.0, ((1, 16), (2, 16))),
        "out_grads": scatter_about(key_of[1], (LAYERS, TOKENS, D), 1.0, 6.0, ((1, 16), (2, 16))),
        "factor_in": scatter_about(key_of[2], (LAYERS, D, D), 0.5, 3.0, ((1, 16), (2, 16)), jnp.float32),
        "factor_out": scatter_about(key_of[3], (LAYERS, D, D), 0.5, 3.0, ((1, 16), (2, 16)), jnp.float32),
        "basis_in": scatter_about(key_of[4], (LAYERS, D, D), D ** -0.5, 0.125, ((1, 16),)),
        "basis_out": scatter_about(key_of[5], (LAYERS, D, D), D ** -0.5, 0.125, ((1, 16),)),
        "eig_in": jnp.clip(jnp.exp(math.log(1.0) - 4.6051702 * jax.random.uniform(key_of[6], (LAYERS, D), jnp.float32) ** level_of(key_of[6], (LAYERS, D), ((1, 16),), -0.2, 0.2)), 0.01, 1.0),
        "eig_out": jnp.clip(jnp.exp(math.log(1.0) - 4.6051702 * jax.random.uniform(key_of[7], (LAYERS, D), jnp.float32) ** level_of(key_of[7], (LAYERS, D), ((1, 16),), -0.2, 0.2)), 0.01, 1.0),
    }


decay = 0.5
damping = 0.001


def reference(acts, out_grads, factor_in, factor_out, basis_in, basis_out, eig_in, eig_out):
    new_in = []
    new_out = []
    results = []
    for layer in range(LAYERS):
        act_rows = acts[layer]
        grad_rows = out_grads[layer]
        cov_in = jnp.dot(act_rows.T, act_rows, preferred_element_type=jnp.float32) / TOKENS
        cov_out = jnp.dot(grad_rows.T, grad_rows, preferred_element_type=jnp.float32) / TOKENS
        new_in.append(decay * factor_in[layer] + (1.0 - decay) * cov_in)
        new_out.append(decay * factor_out[layer] + (1.0 - decay) * cov_out)
        weight_grad = jnp.dot(act_rows.T, grad_rows, preferred_element_type=jnp.float32) / TOKENS
        mixed = jnp.dot(weight_grad, basis_out[layer].astype(jnp.float32), precision=lax.Precision.HIGHEST).astype(jnp.bfloat16)
        eigen = jnp.dot(basis_in[layer].T, mixed, preferred_element_type=jnp.float32)
        scale = 1.0 / (eig_in[layer][:, None] * eig_out[layer][None, :] + damping)
        scaled = (eigen * scale).astype(jnp.bfloat16)
        back = jnp.dot(scaled, basis_out[layer].T, preferred_element_type=jnp.float32).astype(jnp.bfloat16)
        results.append(jnp.dot(basis_in[layer], back, preferred_element_type=jnp.float32).astype(jnp.bfloat16))
    return jnp.stack(new_in), jnp.stack(new_out), jnp.stack(results)
```

```python
import jax
import jax.numpy as jnp
from jax import lax
from jax.sharding import Mesh, PartitionSpec as P

decay = 0.5
damping = 0.001
DP = ("yh", "yl", "xl", "c")
GRAD = ("xh", "z")
bf16 = jnp.bfloat16
f32 = jnp.float32


def dot(left, right, contract):
    return lax.dot_general(left, right, ((contract[:1], contract[1:]), ((), ())), preferred_element_type=f32)


def shift(value, axis, step):
    size = lax.axis_size(axis)
    return lax.ppermute(value, axis, [(i, (i + step) % size) for i in range(size)])


def ring(own):
    size = lax.axis_size("z")
    blocks = {0: own}
    up, down = own, own
    for step in range(1, size // 2 + 1):
        down = shift(down, "z", -1)
        blocks[step] = down
        if step < size - size // 2:
            up = shift(up, "z", 1)
            blocks[-step] = up
    return [blocks[k % size if k % size <= size // 2 else k % size - size] for k in range(size)]


def reorder(parts):
    stacked = jnp.stack(parts)
    size = stacked.shape[0]
    z = lax.axis_index("z")
    twice = jnp.concatenate([stacked, stacked], axis=0)
    return lax.dynamic_slice_in_dim(twice, (size - z) % size, size, axis=0)


def both(own):
    other = shift(own, "xh", 1)
    first = lax.axis_index("xh") == 0
    return jnp.concatenate([jnp.where(first, own, other), jnp.where(first, other, own)], axis=0)


def swap(value):
    pairs = [(a * 2 + b, b * 2 + a) for a in range(2) for b in range(2)]
    return lax.ppermute(value, ("yh", "xh"), pairs)


def exchange_sum(partial, axes, axis):
    count = lax.axis_size(axes)
    got = lax.all_to_all(partial.astype(bf16), axes, axis, axis, tiled=True)
    shape = got.shape
    got = got.reshape(shape[:axis] + (count, shape[axis] // count) + shape[axis + 1 :])
    return jnp.sum(got.astype(f32), axis=axis)


def body(acts, out_grads, factor_in, factor_out, basis_in, basis_out, eig_in, eig_out):
    total_tokens = acts.shape[1] * lax.axis_size(DP)
    width = acts.shape[2]
    act = acts[0].T
    grad = out_grads[0].T
    slab_in = basis_in[0]
    slab_out = basis_out[0]

    act_ring = ring(act)
    grad_pair = both(grad)
    act_pair = both(act)

    def products(pair, blocks):
        parts = [dot(pair, block, (1, 1)).astype(bf16).reshape(2, width, width) for block in blocks]
        ordered = reorder(parts)
        return ordered.transpose(1, 0, 2, 3).reshape(-1, width, width)

    weight = exchange_sum(products(grad_pair, act_ring), DP, 0)[0]
    weight = swap((weight * (1.0 / total_tokens)).astype(bf16))

    mixed = exchange_sum(dot(weight, slab_out, (0, 0)), GRAD, 1).astype(bf16)
    eigen = exchange_sum(dot(mixed, slab_in, (0, 0)), DP, 1)
    scale = 1.0 / (eig_out[0][:, None] * eig_in[0][None, :] + damping)
    scaled = (eigen * scale).astype(bf16)
    scaled_full = lax.all_gather(scaled, GRAD, axis=0, tiled=True)
    back = dot(scaled_full, slab_out, (0, 1)).astype(bf16)
    back_full = lax.all_gather(back, DP, axis=0, tiled=True)
    precond = dot(slab_in, back_full, (1, 0)).astype(bf16)

    def factor(old, pair, blocks):
        part = products(pair, blocks)
        cov = lax.psum_scatter(part.reshape(-1, width), DP, scatter_dimension=0, tiled=True)
        cov = swap(cov).T.astype(f32)
        return (decay * old[0] + ((1.0 - decay) / total_tokens) * cov)[None]

    new_in = factor(factor_in, act_pair, act_ring)
    new_out = factor(factor_out, grad_pair, ring(grad))
    return new_in, new_out, precond[None]


def solution(mesh):
    fine = Mesh(mesh.devices.reshape(2, 2, 2, 2, 2, 8), ("yh", "yl", "xl", "c", "xh", "z"))
    block = P(None, DP, GRAD)
    placed = (block, block, block, block, P(None, DP, None), P(None, GRAD, None), P(None, DP), P(None, GRAD))
    return jax.shard_map(body, mesh=fine, in_specs=placed, out_specs=(block, block, block), check_vma=False)
```

```python
import functools

import jax
import jax.numpy as jnp
from jax import lax
from jax.experimental import pallas as pl
from jax.experimental.pallas import tpu as pltpu
from jax.sharding import Mesh, PartitionSpec as P

decay = 0.5
damping = 0.001
AXES = ("y", "xl", "c", "xh", "z")
DP = ("y", "xl", "c")
GRAD = ("xh", "z")
ROW = ("xh", "y", "xl")
COL = ("z", "c")
bf16 = jnp.bfloat16
f32 = jnp.float32


def dot(left, right, contract):
    return lax.dot_general(left, right, ((contract[:1], contract[1:]), ((), ())), preferred_element_type=f32)


def pack(rest):
    rows = rest.shape[0] // 4
    return jnp.concatenate([rest[rows * q : rows * (q + 1)] for q in range(4)], axis=1)


def unpack(value):
    rows, lanes = value.shape[0] * 4 // 5, value.shape[1]
    part = lanes // 4
    rest = jnp.concatenate([value[rows:, part * q : part * (q + 1)] for q in range(4)], axis=0)
    return jnp.concatenate([value[:rows], rest], axis=1)


class Emit:
    def __init__(self, out, slots, sems):
        self.out, self.slots, self.sems, self.copies = out, slots, sems, []

    def send(self, slot, index):
        number = len(self.copies)
        copy = pltpu.make_async_copy(self.slots.at[slot], self.out.at[index], self.sems.at[number])
        copy.start()
        self.copies.append(copy)

    def put(self, index, value):
        slot = len(self.copies)
        self.slots[slot] = value.astype(self.slots.dtype)
        self.send(slot, index)

    def parts(self, index, main, rest):
        slot = len(self.copies)
        rows = main.shape[0]
        self.slots[slot, :rows] = main.astype(bf16)
        self.slots[slot, rows:] = pack(rest).astype(bf16)
        self.send(slot, index)

    def __call__(self, index, value):
        self.parts(index, value[:, :128], value[:, 128:])

    def everywhere(self, value):
        self(0, value)
        for index in range(1, self.out.shape[0]):
            self.send(0, index)


def call(kernel, ins, outs, after=(), small=(), alias=(), scratch=(), flops=0):
    n, s, a, t, o = len(ins), len(small), len(alias), len(after), len(outs)

    def wrapped(*refs):
        in_refs, small_refs = refs[:n], refs[n : n + s]
        rest = refs[n + s + a + t :]
        out_refs, rest = rest[:o], rest[o:]
        held, in_sems, rest = rest[:n], rest[n], rest[n + 1 :]
        copies = [pltpu.make_async_copy(in_refs[k], held[k], in_sems.at[k]) for k in range(n)]
        for copy in copies:
            copy.start()
        waited = set()

        def get(k):
            if k not in waited:
                copies[k].wait()
                waited.add(k)
            return held[k]

        emits = [Emit(out_refs[k], rest[2 * k], rest[2 * k + 1]) for k in range(o)]
        kernel(get, small_refs, *emits, *rest[2 * o :])
        for k in range(n):
            get(k)
        for emit in emits:
            for copy in emit.copies:
                copy.wait()

    hbm, vmem = pl.BlockSpec(memory_space=pltpu.HBM), pl.BlockSpec(memory_space=pltpu.VMEM)
    space = [pltpu.VMEM(x.shape, x.dtype) for x in ins] + [pltpu.SemaphoreType.DMA((n,))]
    for shape, slots, dtype in outs:
        space += [pltpu.VMEM((slots,) + shape[1:], dtype), pltpu.SemaphoreType.DMA((max(slots, shape[0]),))]
    size = sum(x.size * x.dtype.itemsize for x in ins)
    return pl.pallas_call(
        wrapped,
        out_shape=[jax.ShapeDtypeStruct(shape, dtype) for shape, _, dtype in outs],
        in_specs=[hbm] * n + [vmem] * s + [hbm] * (a + t),
        out_specs=[hbm] * o,
        scratch_shapes=space + [pltpu.VMEM(shape, dtype) for shape, dtype in scratch],
        input_output_aliases={n + s + k: k for k in range(a)},
        compiler_params=pltpu.CompilerParams(vmem_limit_bytes=20 * 2**20),
        cost_estimate=pl.CostEstimate(flops=flops, bytes_accessed=size, transcendentals=0),
    )(*ins, *small, *alias, *after)


def shift(value, axis, step):
    size = lax.axis_size(axis)
    return lax.ppermute(value, axis, [(i, (i + step) % size) for i in range(size)])


def exchange(chunks, axes):
    return lax.all_to_all(chunks, axes, 0, 0, tiled=True)


def pairs_of(there):
    pairs = []
    for y in range(4):
        for xl in range(2):
            for c in range(2):
                for xh in range(2):
                    for z in range(8):
                        here = (((y * 2 + xl) * 2 + c) * 2 + xh) * 8 + z
                        to = there(y, xl, c, xh, z)
                        if to is not None:
                            pairs.append((here, to))
    return pairs


def to_output(y, xl, c, xh, z):
    return (xh * 8 + y * 2 + xl) * 16 + c * 8 + z


def cross_core(y, xl, c, xh, z):
    return (((y * 2 + xl) * 2 + xh) * 2 + c) * 8 + z


def swapped(y, xl, c, xh, z):
    return ((((xh * 2 + y % 2) * 2 + xl) * 2 + c) * 2 + y // 2) * 8 + z


def window_place(transposed):
    def there(y, xl, c, xh, z):
        cross, distance = y // 2, (y % 2 * 2 + xl) * 2 + c
        if distance > 4 or (transposed and distance not in (1, 2, 3)):
            return None
        row = ((xh + cross) % 2) * 8 + (z - 2) % 8
        column = xh * 8 + (z - 2 + distance) % 8
        return column * 16 + row if transposed else row * 16 + column

    return there


def order(*values):
    return lax.optimization_barrier(values)


def body(acts, out_grads, factor_in, factor_out, basis_in, basis_out, eig_in, eig_out):
    total_tokens = acts.shape[1] * lax.axis_size(DP)
    width = acts.shape[2]
    full = basis_in.shape[2]
    count = full // width
    rest = width - 128
    square = (width, width)
    packed = (width * width // 128, 128)
    chunked = (count,) + packed
    act, grad = acts[0].T, out_grads[0].T
    square_flops = 2 * count * width**3
    pair_flops = 2 * width * width * act.shape[1]
    half = width // 2

    def reorder_kernel(get, small, *outs):
        for which, out in enumerate(outs):
            for k in range(count):
                start = k * width
                out.slots[0, :, k * 128 : (k + 1) * 128] = get(which)[:, start : start + 128]
            for k in range(0, count, 4):
                pieces = [get(which)[:, q * width + 128 : (q + 1) * width] for q in range(k, k + 4)]
                out.slots[0, :, count * 128 + k * rest : count * 128 + (k + 4) * rest] = jnp.concatenate(pieces, axis=1)
            out.send(0, 0)

    up1, down1 = shift(act, "z", 1), shift(act, "z", -1)
    grad_flip = shift(grad, "xh", 1)
    act_flip = shift(act, "xh", 1)
    rows = call(reorder_kernel, [basis_out[0], basis_in[0]], [((1, width, full), 1, bf16)] * 2)
    up1, down1, rows_out, rows_in = order(up1, down1, *rows)
    up2, down2 = shift(up1, "z", 1), shift(down1, "z", -1)
    rows_out = lax.ppermute(rows_out[0], AXES, pairs_of(cross_core))
    rows_in = lax.ppermute(rows_in[0], AXES, [(b, a) for a, b in pairs_of(to_output)])
    up2, down2, grad_flip, act_flip = order(up2, down2, grad_flip, act_flip)
    up3, down3 = shift(up2, "z", 1), shift(down2, "z", -1)

    def products(blocks, alias=(), after=()):
        pieces = [piece for parts in blocks.values() for piece in parts]
        own = [k for k, piece in enumerate(pieces) if piece is act]
        moved = [piece for piece in pieces if piece is not act]

        def kernel(get, small, weight_out, cov_out):
            z, xh = lax.axis_index("z"), lax.axis_index("xh")
            at = 0
            for distance, parts in blocks.items():
                place = lax.rem(z + distance, 8)
                if distance:
                    held = [small[at + k][...] for k in range(len(parts))]
                    at += len(parts)
                else:
                    held = [get(0)[...]]

                def product(right):
                    values = [dot(piece, get(right)[...], (1, 1)) for piece in held]
                    return values[0] if len(values) == 1 else jnp.concatenate(values, axis=0)

                weight_out(place * 2 + xh, product(2))
                weight_out(place * 2 + 1 - xh, product(3))
                cov_out(xh * 8 + place, product(0))
                cov_out((1 - xh) * 8 + place, product(1))

        shapes = [(chunked, 2 * len(blocks), bf16)] * 2
        flops = 4 * len(blocks) * pair_flops
        return call(kernel, [act, act_flip, grad, grad_flip], shapes, after, moved, alias, flops=flops)

    parts = products({0: [act], 1: [down1], 7: [up1], 2: [down2], 6: [up2]})
    up3, down3, rows_out, rows_in, *parts = order(up3, down3, rows_out, rows_in, *parts)
    down4, up4 = shift(down3[:half], "z", -1), shift(up3[half:], "z", 1)
    parts = products({3: [down3], 5: [up3]}, parts)
    weight_parts, in_parts = products({4: [down4, up4]}, parts)

    grad_late, weight_parts = order(grad, weight_parts)
    grad_up1, grad_down1 = shift(grad_late, "z", 1), shift(grad_late, "z", -1)
    eigs = lax.ppermute(
        jnp.concatenate([eig_in, eig_out], axis=0), AXES, [(b, a) for a, b in pairs_of(to_output)]
    )

    def total_of(got):
        total = got[0].astype(f32)
        for k in range(1, count):
            total = total + got[k].astype(f32)
        return unpack(total)

    def wide(value, rows_ref, out, index):
        for k in range(0, count, 4):
            main = dot(value, rows_ref[:, k * 128 : (k + 4) * 128], (1, 0))
            start = count * 128 + k * rest
            others = dot(value, rows_ref[:, start : start + 4 * rest], (1, 0))
            for q in range(4):
                out.parts(index(k + q), main[:, q * 128 : (q + 1) * 128], others[:, q * rest : (q + 1) * rest])

    def stacked(got, whole, block):
        for k in range(count):
            value = unpack(got[k].astype(f32)).astype(bf16)
            j = block(k)
            whole[j * 128 : (j + 1) * 128] = value[:128]
            whole[count * 128 + j * rest : count * 128 + (j + 1) * rest] = value[128:]
        return whole[...]

    got = exchange(weight_parts, DP)
    got, grad_up1, grad_down1, in_parts, eigs = order(got, grad_up1, grad_down1, in_parts, eigs)

    def weight_kernel(get, small, out):
        value = (total_of(get(0)) * (1.0 / total_tokens)).astype(bf16)
        wide(value, get(1), out, lambda k: k % 8 * 2 + k // 8)

    (mixed,) = call(weight_kernel, [got, rows_out], [(chunked, count, bf16)], flops=square_flops)
    got = exchange(mixed, COL)
    got, grad_up1, grad_down1 = order(got, grad_up1, grad_down1)

    def mixed_kernel(get, small, out):
        wide(total_of(get(0)).T.astype(bf16), get(1), out, lambda k: k)

    (eigen,) = call(mixed_kernel, [got, rows_in], [(chunked, count, bf16)], flops=square_flops)
    grad_up2, grad_down2 = shift(grad_up1, "z", 1), shift(grad_down1, "z", -1)
    got = exchange(eigen, ROW)
    got, grad_up2, grad_down2 = order(got, grad_up2, grad_down2)
    grad_cross = shift(grad_up2, "xh", 1)

    def eigen_kernel(get, small, out):
        eigs_ref, column_ref = small
        scale = 1.0 / (column_ref[...] * eigs_ref[0:1, :] + damping)
        out(0, total_of(get(0)) * scale)

    (scaled,) = call(eigen_kernel, [got], [((1,) + packed, 1, bf16)], (), [eigs, eigs[1][:, None]])
    scaled = lax.all_gather(scaled, COL, axis=0, tiled=True)

    def back_kernel(get, small, out, whole):
        value = dot(get(1)[...], stacked(get(0), whole, lambda k: k % 2 * 8 + k // 2), (1, 0))
        out.everywhere(value.T)

    space = [((full, width), bf16)]
    (back,) = call(back_kernel, [scaled, rows_out], [(chunked, 1, bf16)], (), (), (), space, square_flops)
    back = exchange(back, ROW)

    def cov_kernel(get, small, out):
        for cross in range(2):
            for distance in range(8):
                if distance < 5:
                    out(cross * 8 + distance, dot(get(5 if cross else 0)[...], get(distance)[...], (1, 1)))
                else:
                    out(cross * 8 + distance, jnp.zeros(square, f32))

    window = [grad_up2, grad_up1, grad_late, grad_down1, grad_down2, grad_cross]
    (out_parts,) = call(cov_kernel, window, [(chunked, count, bf16)], flops=10 * pair_flops)
    back, out_parts = order(back, out_parts)

    def last_kernel(get, small, out, whole):
        out.put(0, dot(get(1)[...], stacked(get(0), whole, lambda k: k), (1, 0)))

    (precond,) = call(
        last_kernel, [back, rows_in], [((1,) + square, 1, bf16)], (), (), (), space, square_flops
    )
    precond = lax.ppermute(precond, AXES, pairs_of(to_output))

    def unpack_kernel(get, small, out):
        out.put(0, unpack(get(0)[...].astype(f32)))

    new_in = lax.psum_scatter(in_parts.reshape(-1, 128), DP, scatter_dimension=0, tiled=True)
    (new_in,) = call(unpack_kernel, [new_in], [((1,) + square, 1, bf16)])
    new_in = lax.ppermute(new_in, AXES, pairs_of(swapped)).astype(f32)

    def sum_kernel(get, small, out):
        out.put(0, total_of(get(0)))

    (out_cov,) = call(sum_kernel, [exchange(out_parts, DP)], [((1,) + square, 1, bf16)])
    new_out = lax.ppermute(out_cov, AXES, pairs_of(window_place(False))).astype(f32)
    new_out = new_out + lax.ppermute(out_cov, AXES, pairs_of(window_place(True))).astype(f32).transpose(0, 2, 1)

    def factor(old, cov):
        return decay * old + ((1.0 - decay) / total_tokens) * cov

    return factor(factor_in, new_in), factor(factor_out, new_out), precond


def solution(mesh):
    fine = Mesh(mesh.devices.reshape(4, 2, 2, 2, 8), AXES)
    block = P(None, DP, GRAD)
    placed = (block, block, block, block, P(None, DP, None), P(None, GRAD, None), P(None, DP), P(None, GRAD))
    return jax.shard_map(body, mesh=fine, in_specs=placed, out_specs=(block, block, block), check_vma=False)
```

```python
import functools

import jax
import jax.numpy as jnp
from jax import lax
from jax.experimental import pallas as pl
from jax.experimental.pallas import tpu as pltpu
from jax.sharding import Mesh, PartitionSpec as P

decay = 0.5
damping = 0.001
AXES = ("y", "xl", "c", "xh", "z")
DP = ("y", "xl", "c")
GRAD = ("xh", "z")
ROW = ("xh", "y", "xl")
COL = ("z", "c")
bf16 = jnp.bfloat16
f32 = jnp.float32


def dot(left, right, contract):
    return lax.dot_general(left, right, ((contract[:1], contract[1:]), ((), ())), preferred_element_type=f32)


def pack(rest):
    rows = rest.shape[0] // 4
    return jnp.concatenate([rest[rows * q : rows * (q + 1)] for q in range(4)], axis=1)


def unpack(value):
    rows, lanes = value.shape[0] * 4 // 5, value.shape[1]
    part = lanes // 4
    rest = jnp.concatenate([value[rows:, part * q : part * (q + 1)] for q in range(4)], axis=0)
    return jnp.concatenate([value[:rows], rest], axis=1)


class Emit:
    def __init__(self, out, slots, sems):
        self.out, self.slots, self.sems, self.copies = out, slots, sems, []

    def send(self, slot, index):
        number = len(self.copies)
        copy = pltpu.make_async_copy(self.slots.at[slot], self.out.at[index], self.sems.at[number])
        copy.start()
        self.copies.append(copy)

    def put(self, index, value):
        slot = len(self.copies)
        self.slots[slot] = value.astype(self.slots.dtype)
        self.send(slot, index)

    def parts(self, index, main, rest):
        slot = len(self.copies)
        rows = main.shape[0]
        self.slots[slot, :rows] = main.astype(bf16)
        self.slots[slot, rows:] = pack(rest).astype(bf16)
        self.send(slot, index)

    def __call__(self, index, value):
        self.parts(index, value[:, :128], value[:, 128:])

    def everywhere(self, value):
        self(0, value)
        for index in range(1, self.out.shape[0]):
            self.send(0, index)


def call(kernel, ins, outs, after=(), small=(), alias=(), scratch=(), flops=0):
    n, s, a, t, o = len(ins), len(small), len(alias), len(after), len(outs)

    def wrapped(*refs):
        in_refs, small_refs = refs[:n], refs[n : n + s]
        rest = refs[n + s + a + t :]
        out_refs, rest = rest[:o], rest[o:]
        held, in_sems, rest = rest[:n], rest[n], rest[n + 1 :]
        copies = [pltpu.make_async_copy(in_refs[k], held[k], in_sems.at[k]) for k in range(n)]
        for copy in copies:
            copy.start()
        waited = set()

        def get(k):
            if k not in waited:
                copies[k].wait()
                waited.add(k)
            return held[k]

        emits = [Emit(out_refs[k], rest[2 * k], rest[2 * k + 1]) for k in range(o)]
        kernel(get, small_refs, *emits, *rest[2 * o :])
        for k in range(n):
            get(k)
        for emit in emits:
            for copy in emit.copies:
                copy.wait()

    hbm, vmem = pl.BlockSpec(memory_space=pltpu.HBM), pl.BlockSpec(memory_space=pltpu.VMEM)
    space = [pltpu.VMEM(x.shape, x.dtype) for x in ins] + [pltpu.SemaphoreType.DMA((max(n, 1),))]
    for shape, slots, dtype in outs:
        space += [pltpu.VMEM((slots,) + shape[1:], dtype), pltpu.SemaphoreType.DMA((max(slots, shape[0]),))]
    size = sum(x.size * x.dtype.itemsize for x in ins)
    return pl.pallas_call(
        wrapped,
        out_shape=[jax.ShapeDtypeStruct(shape, dtype) for shape, _, dtype in outs],
        in_specs=[hbm] * n + [vmem] * s + [hbm] * (a + t),
        out_specs=[hbm] * o,
        scratch_shapes=space + [pltpu.VMEM(shape, dtype) for shape, dtype in scratch],
        input_output_aliases={n + s + k: k for k in range(a)},
        compiler_params=pltpu.CompilerParams(vmem_limit_bytes=20 * 2**20),
        cost_estimate=pl.CostEstimate(flops=flops, bytes_accessed=size, transcendentals=0),
    )(*ins, *small, *alias, *after)


def shift(value, axis, step):
    size = lax.axis_size(axis)
    return lax.ppermute(value, axis, [(i, (i + step) % size) for i in range(size)])


def exchange(chunks, axes):
    return lax.all_to_all(chunks, axes, 0, 0, tiled=True)


def pairs_of(there):
    pairs = []
    for y in range(4):
        for xl in range(2):
            for c in range(2):
                for xh in range(2):
                    for z in range(8):
                        here = (((y * 2 + xl) * 2 + c) * 2 + xh) * 8 + z
                        to = there(y, xl, c, xh, z)
                        if to is not None:
                            pairs.append((here, to))
    return pairs


def to_output(y, xl, c, xh, z):
    return (xh * 8 + y * 2 + xl) * 16 + c * 8 + z


def cross_core(y, xl, c, xh, z):
    return (((y * 2 + xl) * 2 + xh) * 2 + c) * 8 + z


def swapped(y, xl, c, xh, z):
    return ((((xh * 2 + y % 2) * 2 + xl) * 2 + c) * 2 + y // 2) * 8 + z


def window_place(transposed):
    def there(y, xl, c, xh, z):
        cross, distance = y // 2, (y % 2 * 2 + xl) * 2 + c
        if distance > 4 or (transposed and distance not in (1, 2, 3)):
            return None
        row = ((xh + cross) % 2) * 8 + (z - 2) % 8
        column = xh * 8 + (z - 2 + distance) % 8
        return column * 16 + row if transposed else row * 16 + column

    return there


def order(*values):
    return lax.optimization_barrier(values)


def body(acts, out_grads, factor_in, factor_out, basis_in, basis_out, eig_in, eig_out):
    total_tokens = acts.shape[1] * lax.axis_size(DP)
    width = acts.shape[2]
    full = basis_in.shape[2]
    count = full // width
    rest = width - 128
    square = (width, width)
    packed = (width * width // 128, 128)
    chunked = (count,) + packed
    act, grad = acts[0].T, out_grads[0].T
    square_flops = 2 * count * width**3
    pair_flops = 2 * width * width * act.shape[1]
    half = width // 2

    def reorder_kernel(get, small, *outs):
        for which, out in enumerate(outs):
            for k in range(count):
                start = k * width
                out.slots[0, :, k * 128 : (k + 1) * 128] = get(which)[:, start : start + 128]
            for k in range(0, count, 4):
                pieces = [get(which)[:, q * width + 128 : (q + 1) * width] for q in range(k, k + 4)]
                out.slots[0, :, count * 128 + k * rest : count * 128 + (k + 4) * rest] = jnp.concatenate(pieces, axis=1)
            out.send(0, 0)

    up1, down1 = shift(act, "z", 1), shift(act, "z", -1)
    grad_flip = shift(grad, "xh", 1)
    act_flip = shift(act, "xh", 1)
    rows = call(reorder_kernel, [basis_out[0], basis_in[0]], [((1, width, full), 1, bf16)] * 2)
    up1, down1, rows_out, rows_in = order(up1, down1, *rows)
    up2, down2 = shift(up1, "z", 1), shift(down1, "z", -1)
    rows_out = lax.ppermute(rows_out[0], AXES, pairs_of(cross_core))
    rows_in = lax.ppermute(rows_in[0], AXES, [(b, a) for a, b in pairs_of(to_output)])
    up2, down2, grad_flip, act_flip = order(up2, down2, grad_flip, act_flip)
    up3, down3 = shift(up2, "z", 1), shift(down2, "z", -1)

    def products(blocks, alias=()):
        pieces = [piece for parts in blocks.values() for piece in parts]

        def kernel(get, small, weight_out, cov_out):
            z, xh = lax.axis_index("z"), lax.axis_index("xh")
            y, xl, c = lax.axis_index("y"), lax.axis_index("xl"), lax.axis_index("c")
            at = 4

            def staged(other, place):
                to_y, to_xl, to_c = other * 2 + place // 4, lax.rem(place // 2, 2), lax.rem(place, 2)
                return lax.rem(to_c + c, 2) * 8 + lax.rem(to_xl + xl, 2) * 4 + lax.rem(to_y - y + 4, 4)

            for distance, parts in blocks.items():
                place = lax.rem(z + distance, 8)
                held = [small[at + k][...] for k in range(len(parts))]
                at += len(parts)

                def product(right):
                    values = [dot(piece, small[right][...], (1, 1)) for piece in held]
                    return values[0] if len(values) == 1 else jnp.concatenate(values, axis=0)

                weight_out(place * 2 + xh, product(2))
                weight_out(place * 2 + 1 - xh, product(3))
                cov_out(staged(xh, place), product(0))
                cov_out(staged(1 - xh, place), product(1))

        shapes = [(chunked, 2 * len(blocks), bf16)] * 2
        flops = 4 * len(blocks) * pair_flops
        return call(kernel, [], shapes, (), [act, act_flip, grad, grad_flip, *pieces], alias, flops=flops)

    parts = products({0: [act], 1: [down1], 7: [up1], 2: [down2], 6: [up2]})
    up3, down3, *parts = order(up3, down3, *parts)
    down4, up4 = shift(down3[:half], "z", -1), shift(up3[half:], "z", 1)
    parts = products({3: [down3], 5: [up3]}, parts)
    grad_late, *parts = order(grad, *parts)
    weight_parts, in_parts = products({4: [down4, up4]}, parts)

    grad_up1, grad_down1 = shift(grad_late, "z", 1), shift(grad_late, "z", -1)
    eigs = lax.ppermute(
        jnp.concatenate([eig_in, eig_out], axis=0), AXES, [(b, a) for a, b in pairs_of(to_output)]
    )

    def pair_sum(chunks, axis):
        half = chunks.shape[0] // 2
        other = shift(chunks[half:], axis, 1)

        def kernel(get, small, out):
            for k in range(half):
                out.put(k, get(0)[k].astype(f32) + get(1)[k].astype(f32))

        (total,) = call(kernel, [chunks[:half], other], [((half,) + packed, half, bf16)])
        return total

    def total_of(got):
        total = got[0].astype(f32)
        for k in range(1, got.shape[0]):
            total = total + got[k].astype(f32)
        return unpack(total)

    def wide(value, rows_ref, out, index):
        for k in range(0, count, 4):
            main = dot(value, rows_ref[:, k * 128 : (k + 4) * 128], (1, 0))
            start = count * 128 + k * rest
            others = dot(value, rows_ref[:, start : start + 4 * rest], (1, 0))
            for q in range(4):
                out.parts(index(k + q), main[:, q * 128 : (q + 1) * 128], others[:, q * rest : (q + 1) * rest])

    def stacked(got, whole, block):
        for k in range(got.shape[0]):
            value = unpack(got[k].astype(f32)).astype(bf16)
            j = block(k)
            whole[pl.ds(pl.multiple_of(j * 128, 128), 128)] = value[:128]
            whole[pl.ds(pl.multiple_of(count * 128 + j * rest, rest), rest)] = value[128:]

    got = exchange(weight_parts, DP)
    in_sum = pair_sum(in_parts, "c")
    got, eigs, rows_out, rows_in, grad_up1, grad_down1, in_sum = order(
        got, eigs, rows_out, rows_in, grad_up1, grad_down1, in_sum
    )

    def weight_kernel(get, small, out):
        value = (total_of(get(0)) * (1.0 / total_tokens)).astype(bf16)
        c = lax.axis_index("c")
        wide(value, get(1), out, lambda k: lax.rem(k // 8 + c, 2) * 8 + k % 8)

    (mixed,) = call(weight_kernel, [got, rows_out], [(chunked, count, bf16)], flops=square_flops)
    got = exchange(pair_sum(mixed, "c"), "z")
    in_sum = pair_sum(in_sum, "xl")
    got, in_sum = order(got, in_sum)

    def mixed_kernel(get, small, out):
        wide(total_of(get(0)).T.astype(bf16), get(1), out, lambda k: k)

    (eigen,) = call(mixed_kernel, [got, rows_in], [(chunked, count, bf16)], flops=square_flops)
    grad_up2, grad_down2 = shift(grad_up1, "z", 1), shift(grad_down1, "z", -1)
    got = exchange(eigen, ROW)
    def eigen_kernel(get, small, out):
        eigs_ref, column_ref = small
        scale = 1.0 / (column_ref[...] * eigs_ref[0:1, :] + damping)
        out.everywhere(total_of(get(0)) * scale)

    (scaled,) = call(eigen_kernel, [got], [((count // 2,) + packed, 1, bf16)], (), [eigs, eigs[1][:, None]])
    scaled, grad_up2, grad_down2 = order(scaled, grad_up2, grad_down2)
    grad_cross = shift(grad_up2, "xh", 1)
    scaled = exchange(scaled, "z")
    in_got = [in_sum[0]] + [shift(in_sum[k], "y", k) for k in range(1, 4)]
    scaled, grad_cross, *in_got = order(scaled, grad_cross, *in_got)
    scaled_other = shift(scaled, "c", 1)

    def back_kernel(get, small, out, whole):
        c = lax.axis_index("c")
        stacked(get(0), whole, lambda k: c * 8 + k)
        stacked(get(1), whole, lambda k: (1 - c) * 8 + k)
        out.everywhere(dot(get(2)[...], whole[...], (1, 0)).T)

    space = [((full, width), bf16)]
    (back,) = call(back_kernel, [scaled, scaled_other, rows_out], [(chunked, 1, bf16)], (), (), (), space, square_flops)
    back = exchange(back, ROW)

    def cov_kernel(get, small, out):
        c = lax.axis_index("c")
        for cross in range(2):
            for distance in range(8):
                index = lax.rem(distance + c, 2) * 8 + cross * 4 + distance // 2
                if distance < 5:
                    out(index, dot(get(5 if cross else 0)[...], get(distance)[...], (1, 1)))
                else:
                    out(index, jnp.zeros(square, f32))

    window = [grad_up2, grad_up1, grad_late, grad_down1, grad_down2, grad_cross]
    (out_parts,) = call(cov_kernel, window, [(chunked, count, bf16)], flops=10 * pair_flops)
    out_parts = pair_sum(out_parts, "c")
    back, out_parts = order(back, out_parts)

    def last_kernel(get, small, out, whole):
        stacked(get(0), whole, lambda k: jnp.int32(k))
        out.put(0, dot(get(1)[...], whole[...], (1, 0)))

    (precond,) = call(
        last_kernel, [back, rows_in], [((1,) + square, 1, bf16)], (), (), (), space, square_flops
    )
    precond = lax.ppermute(precond, AXES, pairs_of(to_output))

    def sum_kernel(get, small, out):
        out.put(0, total_of(get(0)))

    def staged_kernel(get, small, out):
        total = get(0)[...].astype(f32)
        for k in range(1, 4):
            total = total + get(k)[...].astype(f32)
        out.put(0, unpack(total))

    (in_cov,) = call(staged_kernel, in_got, [((1,) + square, 1, bf16)])
    in_cov = lax.ppermute(in_cov, AXES, pairs_of(swapped))
    (out_cov,) = call(sum_kernel, [exchange(out_parts, ("y", "xl"))], [((1,) + square, 1, bf16)])
    out_cov = [lax.ppermute(out_cov, AXES, pairs_of(window_place(mirror))) for mirror in (False, True)]

    def factor(old, *covs):
        def kernel(get, small, out):
            cov = small[1][0].astype(f32)
            if len(covs) > 1:
                cov = cov + small[2][0].astype(f32).T
            out.put(0, decay * small[0][0] + ((1.0 - decay) / total_tokens) * cov)

        return call(kernel, [], [(old.shape, 1, f32)], (), [old, *covs])[0]

    return factor(factor_in, in_cov), factor(factor_out, *out_cov), precond


def solution(mesh):
    fine = Mesh(mesh.devices.reshape(4, 2, 2, 2, 8), AXES)
    block = P(None, DP, GRAD)
    placed = (block, block, block, block, P(None, DP, None), P(None, GRAD, None), P(None, DP), P(None, GRAD))
    return jax.shard_map(body, mesh=fine, in_specs=placed, out_specs=(block, block, block), check_vma=False)
```

```python
import functools

import jax
import jax.numpy as jnp
from jax import lax
from jax.experimental import pallas as pl
from jax.experimental.pallas import tpu as pltpu
from jax.sharding import Mesh, PartitionSpec as P

decay = 0.5
damping = 0.001
AXES = ("y", "xl", "c", "xh", "z")
DP = ("y", "xl", "c")
GRAD = ("xh", "z")
ROW = ("xh", "y", "xl")
COL = ("z", "c")
bf16 = jnp.bfloat16
f32 = jnp.float32


def dot(left, right, contract):
    return lax.dot_general(left, right, ((contract[:1], contract[1:]), ((), ())), preferred_element_type=f32)


def pack(rest):
    rows = rest.shape[0] // 4
    return jnp.concatenate([rest[rows * q : rows * (q + 1)] for q in range(4)], axis=1)


def unpack(value):
    rows, lanes = value.shape[0] * 4 // 5, value.shape[1]
    part = lanes // 4
    rest = jnp.concatenate([value[rows:, part * q : part * (q + 1)] for q in range(4)], axis=0)
    return jnp.concatenate([value[:rows], rest], axis=1)


class Emit:
    def __init__(self, out, slots, sems, whole):
        self.out, self.slots, self.sems, self.whole, self.copies = out, slots, sems, whole, []

    def send(self, slot, index):
        number = len(self.copies)
        copy = pltpu.make_async_copy(self.slots.at[slot], self.out.at[index], self.sems.at[number])
        copy.start()
        self.copies.append(copy)

    def place(self, index, main, packed=None):
        slot = index if self.whole else len(self.copies)
        if packed is None:
            self.slots[slot] = main.astype(self.slots.dtype)
        else:
            rows = main.shape[0]
            self.slots[slot, :rows] = main.astype(bf16)
            self.slots[slot, rows:] = packed.astype(bf16)
        if not self.whole:
            self.send(slot, index)

    def put(self, index, value):
        self.place(index, value)

    def parts(self, index, main, rest):
        self.place(index, main, pack(rest))

    def __call__(self, index, value):
        self.parts(index, value[:, :128], value[:, 128:])

    def everywhere(self, value):
        main, packed = value[:, :128].astype(bf16), pack(value[:, 128:]).astype(bf16)
        for index in range(self.out.shape[0]):
            self.place(index, main, packed)

    def finish(self):
        if self.whole:
            copy = pltpu.make_async_copy(self.slots, self.out, self.sems.at[0])
            copy.start()
            self.copies.append(copy)
        for copy in self.copies:
            copy.wait()


def call(kernel, ins, outs, after=(), small=(), alias=(), scratch=(), flops=0):
    n, s, a, t, o = len(ins), len(small), len(alias), len(after), len(outs)

    def wrapped(*refs):
        in_refs, small_refs = refs[:n], refs[n : n + s]
        rest = refs[n + s + a + t :]
        out_refs, rest = rest[:o], rest[o:]
        held, in_sems, rest = rest[:n], rest[n], rest[n + 1 :]
        copies = [pltpu.make_async_copy(in_refs[k], held[k], in_sems.at[k]) for k in range(n)]
        for copy in copies:
            copy.start()
        waited = set()

        def get(k):
            if k not in waited:
                copies[k].wait()
                waited.add(k)
            return held[k]

        emits = [Emit(out_refs[k], rest[2 * k], rest[2 * k + 1], outs[k][1] == outs[k][0][0]) for k in range(o)]
        kernel(get, small_refs, *emits, *rest[2 * o :])
        for k in range(n):
            get(k)
        for emit in emits:
            emit.finish()

    hbm, vmem = pl.BlockSpec(memory_space=pltpu.HBM), pl.BlockSpec(memory_space=pltpu.VMEM)
    space = [pltpu.VMEM(x.shape, x.dtype) for x in ins] + [pltpu.SemaphoreType.DMA((max(n, 1),))]
    for shape, slots, dtype in outs:
        space += [pltpu.VMEM((slots,) + shape[1:], dtype), pltpu.SemaphoreType.DMA((max(slots, shape[0]),))]
    size = sum(x.size * x.dtype.itemsize for x in ins)
    return pl.pallas_call(
        wrapped,
        out_shape=[jax.ShapeDtypeStruct(shape, dtype) for shape, _, dtype in outs],
        in_specs=[hbm] * n + [vmem] * s + [hbm] * (a + t),
        out_specs=[hbm] * o,
        scratch_shapes=space + [pltpu.VMEM(shape, dtype) for shape, dtype in scratch],
        input_output_aliases={n + s + k: k for k in range(a)},
        compiler_params=pltpu.CompilerParams(vmem_limit_bytes=20 * 2**20),
        cost_estimate=pl.CostEstimate(flops=flops, bytes_accessed=size, transcendentals=0),
    )(*ins, *small, *alias, *after)


def shift(value, axis, step):
    size = lax.axis_size(axis)
    return lax.ppermute(value, axis, [(i, (i + step) % size) for i in range(size)])


def exchange(chunks, axes):
    return lax.all_to_all(chunks, axes, 0, 0, tiled=True)


def pairs_of(there):
    pairs = []
    for y in range(4):
        for xl in range(2):
            for c in range(2):
                for xh in range(2):
                    for z in range(8):
                        here = (((y * 2 + xl) * 2 + c) * 2 + xh) * 8 + z
                        to = there(y, xl, c, xh, z)
                        if to is not None:
                            pairs.append((here, to))
    return pairs


def row_of(y, xl):
    return (y & 1) * 4 + xl * 2 + (y >> 1)


def spot_of(block):
    return (block & 1) * 4 + (block >> 2) * 2 + (block >> 1 & 1)


def to_output(y, xl, c, xh, z):
    return (xh * 8 + row_of(y, xl)) * 16 + c * 8 + z


def cross_core(y, xl, c, xh, z):
    return (((y * 2 + xl) * 2 + xh) * 2 + c) * 8 + z


def swapped(y, xl, c, xh, z):
    return ((((xh * 2 + y % 2) * 2 + xl) * 2 + c) * 2 + y // 2) * 8 + z


def window_place(y, xl, c, xh, z):
    cross, distance = y // 2, (y % 2 * 2 + xl) * 2 + c
    row = ((xh + cross) % 2) * 8 + (z - 2) % 8
    column = xh * 8 + (z - 2 + min(distance, 8 - distance)) % 8
    return column * 16 + row if distance > 4 else row * 16 + column


def order(*values):
    return lax.optimization_barrier(values)


def body(acts, out_grads, factor_in, factor_out, basis_in, basis_out, eig_in, eig_out):
    total_tokens = acts.shape[1] * lax.axis_size(DP)
    width = acts.shape[2]
    full = basis_in.shape[2]
    count = full // width
    rest = width - 128
    square = (width, width)
    packed = (width * width // 128, 128)
    chunked = (count,) + packed
    act, grad = acts[0].T, out_grads[0].T
    square_flops = 2 * count * width**3
    pair_flops = 2 * width * width * act.shape[1]
    half = width // 2

    def reorder_kernel(get, small, *outs):
        for which, out in enumerate(outs):
            for k in range(count):
                start = k * width
                out.slots[0, :, k * 128 : (k + 1) * 128] = get(which)[:, start : start + 128]
            for k in range(0, count, 4):
                pieces = [get(which)[:, q * width + 128 : (q + 1) * width] for q in range(k, k + 4)]
                out.slots[0, :, count * 128 + k * rest : count * 128 + (k + 4) * rest] = jnp.concatenate(pieces, axis=1)

    up1, down1 = shift(act, "z", 1), shift(act, "z", -1)
    grad_flip = shift(grad, "xh", 1)
    act_flip = shift(act, "xh", 1)
    rows = call(reorder_kernel, [basis_out[0], basis_in[0]], [((1, width, full), 1, bf16)] * 2)
    up1, down1, rows_out, rows_in = order(up1, down1, *rows)
    up2, down2 = shift(up1, "z", 1), shift(down1, "z", -1)
    rows_out = lax.ppermute(rows_out[0], AXES, pairs_of(cross_core))
    up2, down2, grad_flip, act_flip = order(up2, down2, grad_flip, act_flip)
    up3, down3 = shift(up2, "z", 1), shift(down2, "z", -1)

    def products(blocks, alias=()):
        pieces = [piece for parts in blocks.values() for piece in parts]

        def kernel(get, small, weight_out, cov_out):
            z, xh = lax.axis_index("z"), lax.axis_index("xh")
            y, xl, c = lax.axis_index("y"), lax.axis_index("xl"), lax.axis_index("c")
            at = 4

            def staged(other, place):
                to_y, to_xl, to_c = other * 2 + (place >> 2), place >> 1, place
                return ((to_c ^ c) & 1) * 8 + ((to_xl ^ xl) & 1) * 4 + ((to_y - y) & 3)

            places = {distance: (z + distance) & 7 for distance in blocks}
            steps = {distance: (staged(xh, places[distance]), staged(1 - xh, places[distance])) for distance in blocks}

            for distance, parts in blocks.items():
                place = places[distance]
                held = [small[at + k][...] for k in range(len(parts))]
                at += len(parts)

                def product(right):
                    values = [dot(piece, small[right][...], (1, 1)) for piece in held]
                    return values[0] if len(values) == 1 else jnp.concatenate(values, axis=0)

                weight_out(spot_of(place) * 2 + xh, product(2))
                weight_out(spot_of(place) * 2 + 1 - xh, product(3))
                cov_out(steps[distance][0], product(0))
                cov_out(steps[distance][1], product(1))

        shapes = [(chunked, 2 * len(blocks), bf16)] * 2
        flops = 4 * len(blocks) * pair_flops
        return call(kernel, [], shapes, (), [act, act_flip, grad, grad_flip, *pieces], alias, flops=flops)

    parts = products({0: [act], 1: [down1], 7: [up1], 2: [down2], 6: [up2]})
    rows_in = lax.ppermute(rows_in[0], AXES, [(b, a) for a, b in pairs_of(to_output)])
    up3, down3, rows_out, *parts = order(up3, down3, rows_out, *parts)
    down4, up4 = shift(down3[:half], "z", -1), shift(up3[half:], "z", 1)
    parts = products({3: [down3], 5: [up3]}, parts)
    grad_late, rows_in, *parts = order(grad, rows_in, *parts)
    weight_parts, in_parts = products({4: [down4, up4]}, parts)

    grad_up1, grad_down1 = shift(grad_late, "z", 1), shift(grad_late, "z", -1)
    eigs = lax.ppermute(
        jnp.concatenate([eig_in, eig_out], axis=0), AXES, [(b, a) for a, b in pairs_of(to_output)]
    )

    def pair_sum(chunks, axis):
        half = chunks.shape[0] // 2
        other = shift(chunks[half:], axis, 1)

        def kernel(get, small, out):
            for k in range(half):
                out.put(k, get(0)[k].astype(f32) + get(1)[k].astype(f32))

        (total,) = call(kernel, [chunks[:half], other], [((half,) + packed, half, bf16)])
        return total

    def total_of(got):
        total = got[0].astype(f32)
        for k in range(1, got.shape[0]):
            total = total + got[k].astype(f32)
        return unpack(total)

    def wide(value, rows_ref, out, index):
        for k in range(0, count, 4):
            main = dot(value, rows_ref[:, k * 128 : (k + 4) * 128], (1, 0))
            start = count * 128 + k * rest
            others = dot(value, rows_ref[:, start : start + 4 * rest], (1, 0))
            for q in range(4):
                out.parts(index(k + q), main[:, q * 128 : (q + 1) * 128], others[:, q * rest : (q + 1) * rest])

    def stacked(got, whole, block):
        for k in range(got.shape[0]):
            value = unpack(got[k].astype(f32)).astype(bf16)
            j = block(k)
            first = j * 128
            second = count * 128 + j * rest
            if not isinstance(j, int):
                first, second = pl.multiple_of(first, 128), pl.multiple_of(second, rest)
            whole[pl.ds(first, 128)] = value[:128]
            whole[pl.ds(second, rest)] = value[128:]

    got = exchange(weight_parts, DP)
    in_sum = pair_sum(in_parts, "c")
    got, in_sum = order(got, in_sum)

    def weight_kernel(get, small, out):
        value = (total_of(get(0)) * (1.0 / total_tokens)).astype(bf16)
        c = lax.axis_index("c")
        wide(value, get(1), out, lambda k: (k // 8 ^ c) * 8 + k % 8)

    (mixed,) = call(weight_kernel, [got, rows_out], [(chunked, count, bf16)], flops=square_flops)
    mixed, grad_up1, grad_down1 = order(pair_sum(mixed, "c"), grad_up1, grad_down1)
    got = exchange(mixed, "z")
    in_sum = pair_sum(in_sum, "xl")
    got, in_sum, eigs, grad_up1, grad_down1 = order(got, in_sum, eigs, grad_up1, grad_down1)

    def mixed_kernel(get, small, out):
        wide(total_of(get(0)).T.astype(bf16), get(1), out, lambda k: k // 8 * 8 + spot_of(k % 8))

    (eigen,) = call(mixed_kernel, [got, rows_in], [(chunked, count, bf16)], flops=square_flops)
    grad_up2, grad_down2 = shift(grad_up1, "z", 1), shift(grad_down1, "z", -1)
    got = exchange(eigen, ROW)
    in_got = [in_sum[0]] + [shift(in_sum[k], "y", k) for k in range(1, 4)]
    got, *in_got = order(got, *in_got)
    def eigen_kernel(get, small, out):
        eigs_ref, column_ref = small
        scale = 1.0 / (column_ref[...] * eigs_ref[0:1, :] + damping)
        out.everywhere(total_of(get(0)) * scale)

    (scaled,) = call(eigen_kernel, [got], [((count // 2,) + packed, count // 2, bf16)], (), [eigs, eigs[1][:, None]])
    def staged_kernel(get, small, out):
        total = get(0)[...].astype(f32)
        for k in range(1, 4):
            total = total + get(k)[...].astype(f32)
        out.put(0, unpack(total))

    (in_cov,) = call(staged_kernel, in_got, [((1,) + square, 1, bf16)])

    scaled, grad_up2, grad_down2 = order(scaled, grad_up2, grad_down2)
    grad_cross = shift(grad_up2, "xh", 1)
    scaled = exchange(scaled, "z")
    scaled_other = shift(scaled, "c", 1)

    def back_kernel(get, small, out, whole):
        c = lax.axis_index("c")
        stacked(get(0), whole, lambda k: c * 8 + k)
        stacked(get(1), whole, lambda k: (1 - c) * 8 + k)
        out.everywhere(dot(get(2)[...], whole[...], (1, 0)).T)

    space = [((full, width), bf16)]
    (back,) = call(back_kernel, [scaled, scaled_other, rows_out], [(chunked, count, bf16)], (), (), (), space, square_flops)
    back, grad_cross, in_cov = order(back, grad_cross, in_cov)
    back = exchange(back, ROW)
    in_cov = lax.ppermute(in_cov, AXES, pairs_of(swapped))

    def cov_kernel(get, small, out):
        c = lax.axis_index("c")
        for cross in range(2):
            mirrors = {}
            for distance in range(8):
                index = lax.rem(distance + c, 2) * 8 + cross * 4 + distance // 2
                if distance < 5:
                    value = dot(get(5 if cross else 0)[...], get(distance)[...], (1, 1))
                    out(index, value)
                    mirrors[distance] = value
                else:
                    out(index, mirrors[8 - distance].T)

    window = [grad_up2, grad_up1, grad_late, grad_down1, grad_down2, grad_cross]
    (out_parts,) = call(cov_kernel, window, [(chunked, count, bf16)], flops=10 * pair_flops)
    out_parts = pair_sum(out_parts, "c")
    back, out_parts = order(back, out_parts)

    def last_kernel(get, small, out, whole):
        stacked(get(0), whole, lambda k: k // 8 * 8 + row_of(k % 8 // 2, k % 2))
        out.put(0, dot(get(1)[...], whole[...], (1, 0)))

    (precond,) = call(
        last_kernel, [back, rows_in], [((1,) + square, 1, bf16)], (), (), (), space, square_flops
    )
    precond = lax.ppermute(precond, AXES, pairs_of(to_output))

    def sum_kernel(get, small, out):
        out.put(0, total_of(get(0)))

    out_got, in_cov = order(exchange(out_parts, ("y", "xl")), in_cov)
    (out_cov,) = call(sum_kernel, [out_got], [((1,) + square, 1, bf16)])
    out_cov = lax.ppermute(out_cov, AXES, pairs_of(window_place))

    def factor(old, cov):
        def kernel(get, small, out):
            out.put(0, decay * small[0][0] + ((1.0 - decay) / total_tokens) * small[1][0].astype(f32))

        return call(kernel, [], [(old.shape, 1, f32)], (), [old, cov])[0]

    return factor(factor_in, in_cov), factor(factor_out, out_cov), precond


def solution(mesh):
    fine = Mesh(mesh.devices.reshape(4, 2, 2, 2, 8), AXES)
    block = P(None, DP, GRAD)
    placed = (block, block, block, block, P(None, DP, None), P(None, GRAD, None), P(None, DP), P(None, GRAD))
    return jax.shard_map(body, mesh=fine, in_specs=placed, out_specs=(block, block, block), check_vma=False)
```

```python
import functools

import jax
import jax.numpy as jnp
from jax import lax
from jax.experimental import pallas as pl
from jax.experimental.pallas import tpu as pltpu
from jax.sharding import Mesh, PartitionSpec as P

decay = 0.5
damping = 0.001
AXES = ("y", "xl", "c", "xh", "z")
DP = ("y", "xl", "c")
GRAD = ("xh", "z")
ROW = ("xh", "y", "xl")
COL = ("z", "c")
bf16 = jnp.bfloat16
f32 = jnp.float32


def dot(left, right, contract):
    return lax.dot_general(left, right, ((contract[:1], contract[1:]), ((), ())), preferred_element_type=f32)


def pack(rest):
    rows = rest.shape[0] // 4
    return jnp.concatenate([rest[rows * q : rows * (q + 1)] for q in range(4)], axis=1)


def unpack(value):
    rows, lanes = value.shape[0] * 4 // 5, value.shape[1]
    part = lanes // 4
    rest = jnp.concatenate([value[rows:, part * q : part * (q + 1)] for q in range(4)], axis=0)
    return jnp.concatenate([value[:rows], rest], axis=1)


class Emit:
    def __init__(self, out, slots, sems, whole):
        self.out, self.slots, self.sems, self.whole, self.copies = out, slots, sems, whole, []

    def send(self, slot, index):
        number = len(self.copies)
        copy = pltpu.make_async_copy(self.slots.at[slot], self.out.at[index], self.sems.at[number])
        copy.start()
        self.copies.append(copy)

    def place(self, index, main, packed=None):
        slot = index if self.whole else len(self.copies)
        if packed is None:
            self.slots[slot] = main.astype(self.slots.dtype)
        else:
            rows = main.shape[0]
            self.slots[slot, :rows] = main.astype(bf16)
            self.slots[slot, rows:] = packed.astype(bf16)
        if not self.whole:
            self.send(slot, index)

    def put(self, index, value):
        self.place(index, value)

    def parts(self, index, main, rest):
        self.place(index, main, pack(rest))

    def __call__(self, index, value):
        self.parts(index, value[:, :128], value[:, 128:])

    def everywhere(self, value):
        main, packed = value[:, :128].astype(bf16), pack(value[:, 128:]).astype(bf16)
        for index in range(self.out.shape[0]):
            self.place(index, main, packed)

    def finish(self):
        if self.whole and self.sems is not None:
            copy = pltpu.make_async_copy(self.slots, self.out, self.sems.at[0])
            copy.start()
            self.copies.append(copy)
        for copy in self.copies:
            copy.wait()


def call(kernel, ins, outs, after=(), small=(), alias=(), scratch=(), flops=0, load=False):
    n, s, a, t, o = len(ins), len(small), len(alias), len(after), len(outs)
    loads = n if load else 0

    def wrapped(*refs):
        in_refs, small_refs = refs[:n], refs[n : n + s]
        rest = refs[n + s + a + t :]
        out_refs, rest = rest[:o], rest[o:]
        held, in_sems, rest = rest[:loads], rest[loads], rest[loads + 1 :]
        copies = [pltpu.make_async_copy(in_refs[k], held[k], in_sems.at[k]) for k in range(loads)]
        for copy in copies:
            copy.start()
        waited = set()

        def get(k):
            if not load:
                return in_refs[k]
            if k not in waited:
                copies[k].wait()
                waited.add(k)
            return held[k]

        emits = []
        for k, (shape, slots, _) in enumerate(outs):
            if slots:
                emits.append(Emit(out_refs[k], rest[0], rest[1], slots == shape[0]))
                rest = rest[2:]
            else:
                emits.append(Emit(out_refs[k], out_refs[k], None, True))
        kernel(get, small_refs, *emits, *rest)
        for k in range(loads):
            get(k)
        for emit in emits:
            emit.finish()

    hbm, vmem = pl.BlockSpec(memory_space=pltpu.HBM), pl.BlockSpec(memory_space=pltpu.VMEM)
    space = [pltpu.VMEM(x.shape, x.dtype) for x in ins[:loads]] + [pltpu.SemaphoreType.DMA((max(loads, 1),))]
    for shape, slots, dtype in outs:
        if slots:
            space += [pltpu.VMEM((slots,) + shape[1:], dtype), pltpu.SemaphoreType.DMA((max(slots, shape[0]),))]
    out_specs = [hbm if slots else vmem for _, slots, _ in outs]
    size = sum(x.size * x.dtype.itemsize for x in ins)
    return pl.pallas_call(
        wrapped,
        out_shape=[jax.ShapeDtypeStruct(shape, dtype) for shape, _, dtype in outs],
        in_specs=[hbm if load else vmem] * n + [vmem] * s + out_specs[:a] + [hbm] * t,
        out_specs=out_specs,
        scratch_shapes=space + [pltpu.VMEM(shape, dtype) for shape, dtype in scratch],
        input_output_aliases={n + s + k: k for k in range(a)},
        compiler_params=pltpu.CompilerParams(vmem_limit_bytes=20 * 2**20),
        cost_estimate=pl.CostEstimate(flops=flops, bytes_accessed=size, transcendentals=0),
    )(*ins, *small, *alias, *after)


def shift(value, axis, step):
    size = lax.axis_size(axis)
    return lax.ppermute(value, axis, [(i, (i + step) % size) for i in range(size)])


def exchange(chunks, axes):
    return lax.all_to_all(chunks, axes, 0, 0, tiled=True)


def pairs_of(there):
    pairs = []
    for y in range(4):
        for xl in range(2):
            for c in range(2):
                for xh in range(2):
                    for z in range(8):
                        here = (((y * 2 + xl) * 2 + c) * 2 + xh) * 8 + z
                        to = there(y, xl, c, xh, z)
                        if to is not None:
                            pairs.append((here, to))
    return pairs


def row_of(y, xl):
    return (y & 1) * 4 + xl * 2 + (y >> 1)


def spot_of(block):
    return (block & 1) * 4 + (block >> 2) * 2 + (block >> 1 & 1)


def to_output(y, xl, c, xh, z):
    return (xh * 8 + row_of(y, xl)) * 16 + c * 8 + z


def cross_core(y, xl, c, xh, z):
    return (((y * 2 + xl) * 2 + xh) * 2 + c) * 8 + z


def swapped(y, xl, c, xh, z):
    return ((((xh * 2 + y % 2) * 2 + xl) * 2 + c) * 2 + y // 2) * 8 + z


def window_place(y, xl, c, xh, z):
    cross, distance = y // 2, (y % 2 * 2 + xl) * 2 + c
    row = ((xh + cross) % 2) * 8 + (z - 2) % 8
    column = xh * 8 + (z - 2 + min(distance, 8 - distance)) % 8
    return column * 16 + row if distance > 4 else row * 16 + column


def order(*values):
    return lax.optimization_barrier(values)


def body(acts, out_grads, factor_in, factor_out, basis_in, basis_out, eig_in, eig_out):
    total_tokens = acts.shape[1] * lax.axis_size(DP)
    width = acts.shape[2]
    full = basis_in.shape[2]
    count = full // width
    rest = width - 128
    square = (width, width)
    packed = (width * width // 128, 128)
    chunked = (count,) + packed
    act, grad = acts[0].T, out_grads[0].T
    square_flops = 2 * count * width**3
    pair_flops = 2 * width * width * act.shape[1]
    half = width // 2

    def reorder_kernel(get, small, *outs):
        for which, out in enumerate(outs):
            for k in range(count):
                start = k * width
                out.slots[0, :, k * 128 : (k + 1) * 128] = get(which)[:, start : start + 128]
            for k in range(0, count, 4):
                pieces = [get(which)[:, q * width + 128 : (q + 1) * width] for q in range(k, k + 4)]
                out.slots[0, :, count * 128 + k * rest : count * 128 + (k + 4) * rest] = jnp.concatenate(pieces, axis=1)

    up1, down1 = shift(act, "z", 1), shift(act, "z", -1)
    grad_flip = shift(grad, "xh", 1)
    act_flip = shift(act, "xh", 1)
    rows = call(reorder_kernel, [basis_out[0], basis_in[0]], [((1, width, full), 0, bf16)] * 2, load=True)
    up1, down1, rows_out, rows_in = order(up1, down1, *rows)
    up2, down2 = shift(up1, "z", 1), shift(down1, "z", -1)
    rows_out = lax.ppermute(rows_out[0], AXES, pairs_of(cross_core))
    up2, down2, grad_flip, act_flip = order(up2, down2, grad_flip, act_flip)
    up3, down3 = shift(up2, "z", 1), shift(down2, "z", -1)

    def products(blocks, alias=()):
        pieces = [piece for parts in blocks.values() for piece in parts]

        def kernel(get, small, weight_out, cov_out):
            z, xh = lax.axis_index("z"), lax.axis_index("xh")
            y, xl, c = lax.axis_index("y"), lax.axis_index("xl"), lax.axis_index("c")
            at = 4

            def staged(other, place):
                to_y, to_xl, to_c = other * 2 + (place >> 2), place >> 1, place
                return ((to_c ^ c) & 1) * 8 + ((to_xl ^ xl) & 1) * 4 + ((to_y - y) & 3)

            places = {distance: (z + distance) & 7 for distance in blocks}
            steps = {distance: (staged(xh, places[distance]), staged(1 - xh, places[distance])) for distance in blocks}

            for distance, parts in blocks.items():
                place = places[distance]
                held = [small[at + k][...] for k in range(len(parts))]
                at += len(parts)

                def product(right):
                    values = [dot(piece, small[right][...], (1, 1)) for piece in held]
                    return values[0] if len(values) == 1 else jnp.concatenate(values, axis=0)

                weight_out(spot_of(place) * 2 + xh, product(2))
                weight_out(spot_of(place) * 2 + 1 - xh, product(3))
                cov_out(steps[distance][0], product(0))
                cov_out(steps[distance][1], product(1))

        shapes = [(chunked, 2 * len(blocks), bf16), (chunked, 0, bf16)]
        flops = 4 * len(blocks) * pair_flops
        return call(kernel, [], shapes, (), [act, act_flip, grad, grad_flip, *pieces], alias, flops=flops)

    parts = products({0: [act], 1: [down1], 7: [up1], 2: [down2], 6: [up2]})
    rows_in = lax.ppermute(rows_in[0], AXES, [(b, a) for a, b in pairs_of(to_output)])
    up3, down3, rows_out, *parts = order(up3, down3, rows_out, *parts)
    down4, up4 = shift(down3[:half], "z", -1), shift(up3[half:], "z", 1)
    parts = products({3: [down3], 5: [up3]}, parts)
    grad_late, *parts = order(grad, *parts)
    weight_parts, in_parts = products({4: [down4, up4]}, parts)
    weight_parts, rows_in = order(weight_parts, rows_in)

    grad_up1, grad_down1 = shift(grad_late, "z", 1), shift(grad_late, "z", -1)
    eigs = lax.ppermute(
        jnp.concatenate([eig_in, eig_out], axis=0), AXES, [(b, a) for a, b in pairs_of(to_output)]
    )

    def pair_sum(chunks, axis):
        half = chunks.shape[0] // 2
        other = shift(chunks[half:], axis, 1)

        def kernel(get, small, out):
            for k in range(half):
                out.put(k, get(0)[k].astype(f32) + get(1)[k].astype(f32))

        (total,) = call(kernel, [chunks[:half], other], [((half,) + packed, half, bf16)])
        return total

    def total_of(got):
        total = got[0].astype(f32)
        for k in range(1, got.shape[0]):
            total = total + got[k].astype(f32)
        return unpack(total)

    def wide(value, rows_ref, out, index):
        for k in range(0, count, 4):
            main = dot(value, rows_ref[:, k * 128 : (k + 4) * 128], (1, 0))
            start = count * 128 + k * rest
            others = dot(value, rows_ref[:, start : start + 4 * rest], (1, 0))
            for q in range(4):
                out.parts(index(k + q), main[:, q * 128 : (q + 1) * 128], others[:, q * rest : (q + 1) * rest])

    def stacked(got, whole, block):
        for k in range(got.shape[0]):
            value = unpack(got[k].astype(f32)).astype(bf16)
            j = block(k)
            first = j * 128
            second = count * 128 + j * rest
            if not isinstance(j, int):
                first, second = pl.multiple_of(first, 128), pl.multiple_of(second, rest)
            whole[pl.ds(first, 128)] = value[:128]
            whole[pl.ds(second, rest)] = value[128:]

    got = exchange(weight_parts, DP)
    in_sum = pair_sum(in_parts, "c")
    got, in_sum = order(got, in_sum)

    def weight_kernel(get, small, out):
        value = (total_of(get(0)) * (1.0 / total_tokens)).astype(bf16)
        c = lax.axis_index("c")
        wide(value, get(1), out, lambda k: (k // 8 ^ c) * 8 + k % 8)

    (mixed,) = call(weight_kernel, [got, rows_out], [(chunked, count, bf16)], flops=square_flops)
    mixed, grad_up1, grad_down1 = order(pair_sum(mixed, "c"), grad_up1, grad_down1)
    got = exchange(mixed, "z")
    in_sum = pair_sum(in_sum, "xl")
    got, in_sum, eigs, grad_up1, grad_down1 = order(got, in_sum, eigs, grad_up1, grad_down1)

    def mixed_kernel(get, small, out):
        wide(total_of(get(0)).T.astype(bf16), get(1), out, lambda k: k // 8 * 8 + spot_of(k % 8))

    (eigen,) = call(mixed_kernel, [got, rows_in], [(chunked, count, bf16)], flops=square_flops)
    grad_up2, grad_down2 = shift(grad_up1, "z", 1), shift(grad_down1, "z", -1)
    got = exchange(eigen, ROW)
    def eigen_kernel(get, small, out):
        eigs_ref, column_ref = small
        scale = 1.0 / (column_ref[...] * eigs_ref[0:1, :] + damping)
        out.everywhere(total_of(get(0)) * scale)

    (scaled,) = call(eigen_kernel, [got], [((count // 2,) + packed, count // 2, bf16)], (), [eigs, eigs[1][:, None]])
    grad_cross = shift(grad_up2, "xh", 1)
    scaled = exchange(scaled, "z")
    in_got = [in_sum[0]] + [shift(in_sum[k], "y", k) for k in range(1, 4)]
    scaled, *in_got = order(scaled, *in_got)
    scaled_other = shift(scaled, "c", 1)

    def back_kernel(get, small, out, whole):
        c = lax.axis_index("c")
        stacked(get(0), whole, lambda k: c * 8 + k)
        stacked(get(1), whole, lambda k: (1 - c) * 8 + k)
        out.everywhere(dot(get(2)[...], whole[...], (1, 0)).T)

    space = [((full, width), bf16)]
    (back,) = call(back_kernel, [scaled, scaled_other, rows_out], [(chunked, count, bf16)], (), (), (), space, square_flops)
    def staged_kernel(get, small, out):
        total = get(0)[...].astype(f32)
        for k in range(1, 4):
            total = total + get(k)[...].astype(f32)
        out.put(0, unpack(total))

    (in_cov,) = call(staged_kernel, in_got, [((1,) + square, 0, bf16)])

    back, grad_cross = order(back, grad_cross)
    back = exchange(back, ROW)
    in_cov = lax.ppermute(in_cov, AXES, pairs_of(swapped))

    def cov_kernel(get, small, out):
        c = lax.axis_index("c")
        for cross in range(2):
            mirrors = {}
            for distance in range(8):
                index = lax.rem(distance + c, 2) * 8 + cross * 4 + distance // 2
                if distance < 5:
                    value = dot(get(5 if cross else 0)[...], get(distance)[...], (1, 1))
                    out(index, value)
                    mirrors[distance] = value
                else:
                    out(index, mirrors[8 - distance].T)

    window = [grad_up2, grad_up1, grad_late, grad_down1, grad_down2, grad_cross]
    (out_parts,) = call(cov_kernel, window, [(chunked, 0, bf16)], flops=10 * pair_flops, load=True)
    out_parts = pair_sum(out_parts, "c")
    back, out_parts = order(back, out_parts)

    def last_kernel(get, small, out, whole):
        stacked(get(0), whole, lambda k: k // 8 * 8 + row_of(k % 8 // 2, k % 2))
        out.put(0, dot(get(1)[...], whole[...], (1, 0)))

    (precond,) = call(
        last_kernel, [back, rows_in], [((1,) + square, 0, bf16)], (), (), (), space, square_flops
    )
    precond = lax.ppermute(precond, AXES, pairs_of(to_output))

    def sum_kernel(get, small, out):
        out.put(0, total_of(get(0)))

    out_got = exchange(out_parts, ("y", "xl"))
    (out_cov,) = call(sum_kernel, [out_got], [((1,) + square, 0, bf16)])
    out_cov = lax.ppermute(out_cov, AXES, pairs_of(window_place))

    def factor(old, cov):
        def kernel(get, small, out):
            out.put(0, decay * small[0][0] + ((1.0 - decay) / total_tokens) * small[1][0].astype(f32))

        return call(kernel, [], [(old.shape, 0, f32)], (), [old, cov])[0]

    return factor(factor_in, in_cov), factor(factor_out, out_cov), precond


def solution(mesh):
    fine = Mesh(mesh.devices.reshape(4, 2, 2, 2, 8), AXES)
    block = P(None, DP, GRAD)
    placed = (block, block, block, block, P(None, DP, None), P(None, GRAD, None), P(None, DP), P(None, GRAD))
    return jax.shard_map(body, mesh=fine, in_specs=placed, out_specs=(block, block, block), check_vma=False)
```

```python
import functools

import jax
import jax.numpy as jnp
from jax import lax
from jax.experimental import pallas as pl
from jax.experimental.pallas import tpu as pltpu
from jax.sharding import Mesh, PartitionSpec as P

decay = 0.5
damping = 0.001
AXES = ("y", "xl", "c", "xh", "z")
DP = ("y", "xl", "c")
GRAD = ("xh", "z")
ROW = ("xh", "y", "xl")
COL = ("z", "c")
bf16 = jnp.bfloat16
f32 = jnp.float32


def dot(left, right, contract):
    return lax.dot_general(left, right, ((contract[:1], contract[1:]), ((), ())), preferred_element_type=f32)


SPARE = 48


def pack(rest):
    rows = rest.shape[0] // 4
    zeros = jnp.zeros((SPARE - rows, 4 * rest.shape[1]), rest.dtype)
    return jnp.concatenate([jnp.concatenate([rest[rows * q : rows * (q + 1)] for q in range(4)], axis=1), zeros], axis=0)


def unpack(value):
    rows, part = value.shape[0] - SPARE, value.shape[1] // 4
    rest = value[rows : rows + rows // 4]
    rest = jnp.concatenate([rest[:, part * q : part * (q + 1)] for q in range(4)], axis=0)
    return jnp.concatenate([value[:rows], rest], axis=1)


class Emit:
    def __init__(self, out, slots, sems, whole):
        self.out, self.slots, self.sems, self.whole, self.copies = out, slots, sems, whole, []

    def send(self, slot, index):
        number = len(self.copies)
        copy = pltpu.make_async_copy(self.slots.at[slot], self.out.at[index], self.sems.at[number])
        copy.start()
        self.copies.append(copy)

    def place(self, index, main, packed=None):
        slot = index if self.whole else len(self.copies)
        if packed is None:
            self.slots[slot] = main.astype(self.slots.dtype)
        else:
            rows = main.shape[0]
            self.slots[slot, :rows] = main.astype(bf16)
            self.slots[slot, rows:] = packed.astype(bf16)
        if not self.whole:
            self.send(slot, index)

    def put(self, index, value):
        self.place(index, value)

    def parts(self, index, main, rest):
        self.place(index, main, pack(rest))

    def __call__(self, index, value):
        self.parts(index, value[:, :128], value[:, 128:])

    def everywhere(self, value):
        main, packed = value[:, :128].astype(bf16), pack(value[:, 128:]).astype(bf16)
        for index in range(self.out.shape[0]):
            self.place(index, main, packed)

    def finish(self):
        if self.whole and self.sems is not None:
            copy = pltpu.make_async_copy(self.slots, self.out, self.sems.at[0])
            copy.start()
            self.copies.append(copy)
        for copy in self.copies:
            copy.wait()


def call(kernel, ins, outs, after=(), small=(), alias=(), scratch=(), flops=0, load=False):
    n, s, a, t, o = len(ins), len(small), len(alias), len(after), len(outs)
    loads = n if load else 0

    def wrapped(*refs):
        in_refs, small_refs = refs[:n], refs[n : n + s]
        rest = refs[n + s + a + t :]
        out_refs, rest = rest[:o], rest[o:]
        held, in_sems, rest = rest[:loads], rest[loads], rest[loads + 1 :]
        copies = [pltpu.make_async_copy(in_refs[k], held[k], in_sems.at[k]) for k in range(loads)]
        for copy in copies:
            copy.start()
        waited = set()

        def get(k):
            if not load:
                return in_refs[k]
            if k not in waited:
                copies[k].wait()
                waited.add(k)
            return held[k]

        emits = []
        for k, (shape, slots, _) in enumerate(outs):
            if slots:
                emits.append(Emit(out_refs[k], rest[0], rest[1], slots == shape[0]))
                rest = rest[2:]
            else:
                emits.append(Emit(out_refs[k], out_refs[k], None, True))
        kernel(get, small_refs, *emits, *rest)
        for k in range(loads):
            get(k)
        for emit in emits:
            emit.finish()

    hbm, vmem = pl.BlockSpec(memory_space=pltpu.HBM), pl.BlockSpec(memory_space=pltpu.VMEM)
    space = [pltpu.VMEM(x.shape, x.dtype) for x in ins[:loads]] + [pltpu.SemaphoreType.DMA((max(loads, 1),))]
    for shape, slots, dtype in outs:
        if slots:
            space += [pltpu.VMEM((slots,) + shape[1:], dtype), pltpu.SemaphoreType.DMA((max(slots, shape[0]),))]
    out_specs = [hbm if slots else vmem for _, slots, _ in outs]
    size = sum(x.size * x.dtype.itemsize for x in ins)
    return pl.pallas_call(
        wrapped,
        out_shape=[jax.ShapeDtypeStruct(shape, dtype) for shape, _, dtype in outs],
        in_specs=[hbm if load else vmem] * n + [vmem] * s + out_specs[:a] + [hbm] * t,
        out_specs=out_specs,
        scratch_shapes=space + [pltpu.VMEM(shape, dtype) for shape, dtype in scratch],
        input_output_aliases={n + s + k: k for k in range(a)},
        compiler_params=pltpu.CompilerParams(vmem_limit_bytes=20 * 2**20),
        cost_estimate=pl.CostEstimate(flops=flops, bytes_accessed=size, transcendentals=0),
    )(*ins, *small, *alias, *after)


def shift(value, axis, step):
    size = lax.axis_size(axis)
    return lax.ppermute(value, axis, [(i, (i + step) % size) for i in range(size)])


def exchange(chunks, axes):
    return lax.all_to_all(chunks, axes, 0, 0, tiled=True)


def pairs_of(there):
    pairs = []
    for y in range(4):
        for xl in range(2):
            for c in range(2):
                for xh in range(2):
                    for z in range(8):
                        here = (((y * 2 + xl) * 2 + c) * 2 + xh) * 8 + z
                        to = there(y, xl, c, xh, z)
                        if to is not None:
                            pairs.append((here, to))
    return pairs


def row_of(y, xl):
    return (y & 1) * 4 + xl * 2 + (y >> 1)


def spot_of(block):
    return (block & 1) * 4 + (block >> 2) * 2 + (block >> 1 & 1)


def to_output(y, xl, c, xh, z):
    return (xh * 8 + row_of(y, xl)) * 16 + c * 8 + z


def cross_core(y, xl, c, xh, z):
    return (((y * 2 + xl) * 2 + xh) * 2 + c) * 8 + z


def swapped(y, xl, c, xh, z):
    return ((((xh * 2 + y % 2) * 2 + xl) * 2 + c) * 2 + y // 2) * 8 + z


def window_place(y, xl, c, xh, z):
    cross, distance = y // 2, (y % 2 * 2 + xl) * 2 + c
    row = ((xh + cross) % 2) * 8 + (z - 2) % 8
    column = xh * 8 + (z - 2 + min(distance, 8 - distance)) % 8
    return column * 16 + row if distance > 4 else row * 16 + column


def order(*values):
    return lax.optimization_barrier(values)


def body(acts, out_grads, factor_in, factor_out, basis_in, basis_out, eig_in, eig_out):
    total_tokens = acts.shape[1] * lax.axis_size(DP)
    width = acts.shape[2]
    full = basis_in.shape[2]
    count = full // width
    rest = width - 128
    square = (width, width)
    packed = (width + SPARE, 128)
    chunked = (count,) + packed
    act, grad = acts[0].T, out_grads[0].T
    square_flops = 2 * count * width**3
    pair_flops = 2 * width * width * act.shape[1]
    half = width // 2

    def reorder_kernel(get, small, *outs):
        for which, out in enumerate(outs):
            for k in range(count):
                start = k * width
                out.slots[0, :, k * 128 : (k + 1) * 128] = get(which)[:, start : start + 128]
            for k in range(0, count, 4):
                pieces = [get(which)[:, q * width + 128 : (q + 1) * width] for q in range(k, k + 4)]
                out.slots[0, :, count * 128 + k * rest : count * 128 + (k + 4) * rest] = jnp.concatenate(pieces, axis=1)

    up1, down1 = shift(act, "z", 1), shift(act, "z", -1)
    grad_flip = shift(grad, "xh", 1)
    act_flip = shift(act, "xh", 1)
    rows = call(reorder_kernel, [basis_out[0], basis_in[0]], [((1, width, full), 0, bf16)] * 2, load=True)
    up1, down1, rows_out, rows_in = order(up1, down1, *rows)
    up2, down2 = shift(up1, "z", 1), shift(down1, "z", -1)
    rows_out = lax.ppermute(rows_out[0], AXES, pairs_of(cross_core))
    up2, down2, grad_flip, act_flip = order(up2, down2, grad_flip, act_flip)
    up3, down3 = shift(up2, "z", 1), shift(down2, "z", -1)

    def products(blocks, alias=()):
        pieces = [piece for parts in blocks.values() for piece in parts]

        def kernel(get, small, weight_out, cov_out):
            z, xh = lax.axis_index("z"), lax.axis_index("xh")
            y, xl, c = lax.axis_index("y"), lax.axis_index("xl"), lax.axis_index("c")
            at = 4

            def staged(other, place):
                to_y, to_xl, to_c = other * 2 + (place >> 2), place >> 1, place
                return ((to_c ^ c) & 1) * 8 + ((to_xl ^ xl) & 1) * 4 + ((to_y - y) & 3)

            places = {distance: (z + distance) & 7 for distance in blocks}
            steps = {distance: (staged(xh, places[distance]), staged(1 - xh, places[distance])) for distance in blocks}

            for distance, parts in blocks.items():
                place = places[distance]
                held = [small[at + k][...] for k in range(len(parts))]
                at += len(parts)

                def product(right):
                    values = [dot(piece, small[right][...], (1, 1)) for piece in held]
                    return values[0] if len(values) == 1 else jnp.concatenate(values, axis=0)

                weight_out(spot_of(place) * 2 + xh, product(2))
                weight_out(spot_of(place) * 2 + 1 - xh, product(3))
                cov_out(steps[distance][0], product(0))
                cov_out(steps[distance][1], product(1))

        shapes = [(chunked, 2 * len(blocks), bf16), (chunked, 0, bf16)]
        flops = 4 * len(blocks) * pair_flops
        return call(kernel, [], shapes, (), [act, act_flip, grad, grad_flip, *pieces], alias, flops=flops)

    parts = products({0: [act], 1: [down1], 7: [up1], 2: [down2], 6: [up2]})
    rows_in = lax.ppermute(rows_in[0], AXES, [(b, a) for a, b in pairs_of(to_output)])
    up3, down3, rows_out, *parts = order(up3, down3, rows_out, *parts)
    down4, up4 = shift(down3[:half], "z", -1), shift(up3[half:], "z", 1)
    parts = products({3: [down3], 5: [up3]}, parts)
    grad_late, *parts = order(grad, *parts)
    weight_parts, in_parts = products({4: [down4, up4]}, parts)
    weight_parts, rows_in = order(weight_parts, rows_in)

    grad_up1, grad_down1 = shift(grad_late, "z", 1), shift(grad_late, "z", -1)
    eigs = lax.ppermute(
        jnp.concatenate([eig_in, eig_out], axis=0), AXES, [(b, a) for a, b in pairs_of(to_output)]
    )

    def pair_sum(chunks, axis):
        half = chunks.shape[0] // 2
        other = shift(chunks[half:], axis, 1)

        def kernel(get, small, out):
            for k in range(half):
                out.put(k, get(0)[k].astype(f32) + get(1)[k].astype(f32))

        (total,) = call(kernel, [chunks[:half], other], [((half,) + packed, half, bf16)])
        return total

    def total_of(got):
        total = got[0].astype(f32)
        for k in range(1, got.shape[0]):
            total = total + got[k].astype(f32)
        return unpack(total)

    def wide(value, rows_ref, out, index):
        for k in range(0, count, 4):
            main = dot(value, rows_ref[:, k * 128 : (k + 4) * 128], (1, 0))
            start = count * 128 + k * rest
            others = dot(value, rows_ref[:, start : start + 4 * rest], (1, 0))
            for q in range(4):
                out.parts(index(k + q), main[:, q * 128 : (q + 1) * 128], others[:, q * rest : (q + 1) * rest])

    def stacked(got, whole, block):
        for k in range(got.shape[0]):
            value = unpack(got[k].astype(f32)).astype(bf16)
            j = block(k)
            first = j * 128
            second = count * 128 + j * rest
            if not isinstance(j, int):
                first, second = pl.multiple_of(first, 128), pl.multiple_of(second, rest)
            whole[pl.ds(first, 128)] = value[:128]
            whole[pl.ds(second, rest)] = value[128:]

    got = exchange(weight_parts, DP)
    in_sum = pair_sum(in_parts, "c")
    got, in_sum = order(got, in_sum)

    def weight_kernel(get, small, out):
        value = (total_of(get(0)) * (1.0 / total_tokens)).astype(bf16)
        c = lax.axis_index("c")
        wide(value, get(1), out, lambda k: (k // 8 ^ c) * 8 + k % 8)

    (mixed,) = call(weight_kernel, [got, rows_out], [(chunked, count, bf16)], flops=square_flops)
    mixed, grad_up1, grad_down1 = order(pair_sum(mixed, "c"), grad_up1, grad_down1)
    got = exchange(mixed, "z")
    in_sum = pair_sum(in_sum, "xl")
    got, in_sum, eigs, grad_up1, grad_down1 = order(got, in_sum, eigs, grad_up1, grad_down1)

    def mixed_kernel(get, small, out):
        wide(total_of(get(0)).T.astype(bf16), get(1), out, lambda k: k // 8 * 8 + spot_of(k % 8))

    (eigen,) = call(mixed_kernel, [got, rows_in], [(chunked, count, bf16)], flops=square_flops)
    grad_up2, grad_down2 = shift(grad_up1, "z", 1), shift(grad_down1, "z", -1)
    got = exchange(eigen, ROW)
    def eigen_kernel(get, small, out):
        eigs_ref, column_ref = small
        scale = 1.0 / (column_ref[...] * eigs_ref[0:1, :] + damping)
        out.everywhere(total_of(get(0)) * scale)

    (scaled,) = call(eigen_kernel, [got], [((count // 2,) + packed, count // 2, bf16)], (), [eigs, eigs[1][:, None]])
    grad_cross = shift(grad_up2, "xh", 1)
    scaled = exchange(scaled, "z")
    in_got = [in_sum[0]] + [shift(in_sum[k], "y", k) for k in range(1, 4)]
    scaled, *in_got = order(scaled, *in_got)
    scaled_other = shift(scaled, "c", 1)

    def back_kernel(get, small, out, whole):
        c = lax.axis_index("c")
        stacked(get(0), whole, lambda k: c * 8 + k)
        stacked(get(1), whole, lambda k: (1 - c) * 8 + k)
        out.everywhere(dot(get(2)[...], whole[...], (1, 0)).T)

    space = [((full, width), bf16)]
    (back,) = call(back_kernel, [scaled, scaled_other, rows_out], [(chunked, count, bf16)], (), (), (), space, square_flops)
    def staged_kernel(get, small, out):
        total = get(0)[...].astype(f32)
        for k in range(1, 4):
            total = total + get(k)[...].astype(f32)
        out.put(0, unpack(total))

    (in_cov,) = call(staged_kernel, in_got, [((1,) + square, 0, bf16)])

    back, grad_cross = order(back, grad_cross)
    back = exchange(back, ROW)
    in_cov = lax.ppermute(in_cov, AXES, pairs_of(swapped))

    def cov_kernel(get, small, out):
        c = lax.axis_index("c")
        for cross in range(2):
            mirrors = {}
            for distance in range(8):
                index = lax.rem(distance + c, 2) * 8 + cross * 4 + distance // 2
                if distance < 5:
                    value = dot(get(5 if cross else 0)[...], get(distance)[...], (1, 1))
                    out(index, value)
                    mirrors[distance] = value
                else:
                    out(index, mirrors[8 - distance].T)

    window = [grad_up2, grad_up1, grad_late, grad_down1, grad_down2, grad_cross]
    (out_parts,) = call(cov_kernel, window, [(chunked, 0, bf16)], flops=10 * pair_flops, load=True)
    out_parts = pair_sum(out_parts, "c")
    back, out_parts = order(back, out_parts)

    def last_kernel(get, small, out, whole):
        stacked(get(0), whole, lambda k: k // 8 * 8 + row_of(k % 8 // 2, k % 2))
        out.put(0, dot(get(1)[...], whole[...], (1, 0)))

    (precond,) = call(
        last_kernel, [back, rows_in], [((1,) + square, 0, bf16)], (), (), (), space, square_flops
    )
    precond = lax.ppermute(precond, AXES, pairs_of(to_output))

    def sum_kernel(get, small, out):
        out.put(0, total_of(get(0)))

    out_got = exchange(out_parts, ("y", "xl"))
    (out_cov,) = call(sum_kernel, [out_got], [((1,) + square, 0, bf16)])
    out_cov = lax.ppermute(out_cov, AXES, pairs_of(window_place))

    def factor(old, cov):
        def kernel(get, small, out):
            out.put(0, decay * small[0][0] + ((1.0 - decay) / total_tokens) * small[1][0].astype(f32))

        return call(kernel, [], [(old.shape, 0, f32)], (), [old, cov])[0]

    return factor(factor_in, in_cov), factor(factor_out, out_cov), precond


def solution(mesh):
    fine = Mesh(mesh.devices.reshape(4, 2, 2, 2, 8), AXES)
    block = P(None, DP, GRAD)
    placed = (block, block, block, block, P(None, DP, None), P(None, GRAD, None), P(None, DP), P(None, GRAD))
    return jax.shard_map(body, mesh=fine, in_specs=placed, out_specs=(block, block, block), check_vma=False)
```
